32 devices in a mesh: section: 2 (over core), seq: 2 (over x), table: 8 (over z, y).
Axes of the slice: x: 2, y: 2, z: 4, core: 2. Of those that a mesh axis runs over, the one named last changes fastest.
Arguments:
- table_slab: bfloat16 [8192, 512], P('table'), may hold values from -6 to 6
- request_rows: int32 [16, 512], P(('seq', 'table')), may hold values from 0 to 1023
- owner_counts: int32 [16, 8], P(('seq', 'table')), may hold values from 1 to 64, as said below
- item_slots: int32 [16, 1024], P(('seq', 'table')), may hold values from 0 to 511, as said below
- regroup_counts: int32 [8, 2, 2], P('table'), may hold values from 256 to 768, as said below
- history_lengths: int32 [64, 8], P(('seq', 'table')), may hold values from 1 to 128, 256 in all within a row
- w_proj: bfloat16 [2, 512, 2048], P('section'), may hold values from -0.25 to 0.25
- bias_proj: float32 [2, 2048], P('section'), may hold values from -3 to 3
- gain_in: float32 [2, 512], P('section'), may hold values from 0.5 to 1.5
- gain_mid: float32 [2, 512], P('section'), may hold values from 0.5 to 1.5
- rel_bias: float32 [2, 4, 128], P('section'), may hold values from -4 to 4
- w_out: bfloat16 [2, 512, 512], P('section'), may hold values from -0.25 to 0.25
Outputs:
- states: bfloat16 [2, 16384, 512], P('section', ('seq', 'table'))
The draws below stay inside these ranges and needn't reach their ends.
Inputs may be any that keep to these rules, and one draw needn't show every extreme that they name: `owner_counts`: each block's requests are listed owner by owner; in every set of blocks with one seq index, some owner receives 64 requests from each of them. `item_slots`: every slot lies below the sum of its block's owner_counts. `regroup_counts`: for every table index, each source's and each destination's counts sum to 1024; each source's events are ordered by destination, and a destination lays its events out source after source; every row and every column reaches 768.
All inputs are finite; a program needn't handle non-finite values.
Results may differ from the reference program's by a relative error of at most 0.0064.
Values may be sent and summed in bfloat16 or wider, within the bound.
A program may use at most 64 MiB of HBM per device.

```python
import math
import jax
import jax.numpy as jnp
import numpy as np
from jax import lax

D = 512
HEADS = 4
LMAX = 128
MB_TOK = 256
USERS = 8
TOK_DEV = 1024
CAP = 64
ROWS_DEV = 1024
PROJ = 2048
LAYERS = 2
TABLES = 8
PEERS = 2
EVDEV = 16
MICRO = 4
RQ = 512
ITEMS = 8192


def owner_plan(key):
    base_key = jax.random.fold_in(key, 11)
    count_key, hot_key = jax.random.split(base_key)
    counts = jax.random.randint(count_key, (EVDEV, TABLES), 1, CAP + 1, dtype=jnp.int32)
    hottest = jax.random.randint(hot_key, (PEERS,), 0, TABLES, dtype=jnp.int32)
    device_hot = jnp.repeat(hottest, TABLES)
    columns = jnp.arange(TABLES, dtype=jnp.int32)
    blocks = jnp.arange(EVDEV, dtype=jnp.int32)
    hot = (columns[None, :] == device_hot[:, None]) | (blocks[:, None] == 0)
    return jnp.where(hot, CAP, counts).astype(jnp.int32)


def draw_owner_counts(key, part):
    return owner_plan(key)


def draw_item_slots(key, part):
    totals = jnp.sum(owner_plan(key), axis=1).astype(jnp.int32)
    slot_key = jax.random.fold_in(key, 12)
    slots = jax.random.randint(slot_key, (EVDEV, TOK_DEV), 0, totals[:, None], dtype=jnp.int32)
    return slots.at[:, 0].set(totals - 1).astype(jnp.int32)


def draw_regroup_counts(key, part):
    base_key = jax.random.fold_in(key, 21)
    perm_key, size_key = jax.random.split(base_key)
    baseline = TOK_DEV // PEERS
    swing_size = TOK_DEV // (2 * PEERS)
    orders = jax.vmap(lambda single_key: jax.random.permutation(single_key, PEERS))(jax.random.split(perm_key, TABLES))
    amounts = jax.random.randint(size_key, (TABLES, PEERS // 2), 0, swing_size + 1, dtype=jnp.int32)
    amounts = amounts.at[:, 0].set(swing_size)
    positions = jnp.arange(PEERS, dtype=jnp.int32)
    sign_row = jnp.where(positions % 2 == 0, 1, -1).astype(jnp.int32)
    pattern = amounts[:, positions // 2] * sign_row[None, :]
    shifted = (orders[:, None, :].astype(jnp.int32) - positions[None, :, None]) % PEERS
    spread_out = jnp.broadcast_to(pattern[:, None, :], (TABLES, PEERS, PEERS))
    picked = jnp.take_along_axis(spread_out, shifted, axis=2)
    return (baseline + picked).astype(jnp.int32)


def with_ends(values, key, smallest, top_value):
    longest = values.shape.index(max(values.shape))
    spots = []
    for shift in (0, 1):
        where = [jax.random.randint(jax.random.fold_in(key, axis), (), 0, length) for axis, length in enumerate(values.shape)]
        where[longest] = (where[longest] + shift) % values.shape[longest]
        spots.append(tuple(where))
    return values.at[spots[0]].set(smallest).at[spots[1]].set(top_value)


def block_scale(stream_key, shape, cuts, low, high):
    def one(axis_at, parts):
        draws = jax.random.uniform(jax.random.fold_in(jax.random.fold_in(stream_key, 6), axis_at), (parts,), jnp.float32, low / len(cuts), high / len(cuts))
        return jnp.repeat(jnp.exp(draws), shape[axis_at] // parts).reshape((-1,) + (1,) * (len(shape) - axis_at - 1))

    factor_of = one(*cuts[0])
    for cut in cuts[1:]:
        factor_of = factor_of * one(*cut)
    return factor_of


def profile(number_of, total, limit, slope):
    portions = [(1 << 20) // math.isqrt(grade ** slope) + 1 for grade in range(2, number_of + 1)]
    spare, holding = total - limit - (number_of - 1), [1] * (number_of - 1)
    while spare > 0:
        free = [i for i in range(number_of - 1) if holding[i] < limit]
        pool, budget = sum([portions[i] for i in free]), spare
        for i in free:
            extra = min(limit - holding[i], max(1, budget * portions[i] // pool), spare)
            holding[i] = holding[i] + extra
            spare = spare - extra
    return np.array([limit] + holding)


def uneven_parts(stream_key, amount, total, limit, lean):
    if amount == 2:
        one = jax.random.randint(stream_key, (), max(1, total - limit), min(limit, total - 1) + 1)
        return jnp.stack([one, total - one])
    sizes = jnp.asarray(profile(amount, total, limit, lean), jnp.int32)
    twos = (amount - 1) // 2
    giver, taker = sizes[1:1 + 2 * twos:2], sizes[2:2 + 2 * twos:2]
    room = jnp.minimum(giver - 1, limit - taker)
    moved = jax.random.randint(jax.random.fold_in(stream_key, 1), (twos,), 0, 1 << 20) % (room + 1)
    sizes = sizes.at[1:1 + 2 * twos:2].set(giver - moved).at[2:2 + 2 * twos:2].set(taker + moved)
    return sizes[jax.random.permutation(jax.random.fold_in(stream_key, 2), amount)]


def centred(key, extent, width, bound, cuts=(), held_as=jnp.bfloat16):
    level = block_scale(key, extent, cuts, -0.22, 0.18) if cuts else 1.0
    drawn = jax.random.normal(key, extent, jnp.float32) * width * level
    return jnp.minimum(jnp.maximum(drawn, -bound), bound).astype(held_as)


def setup_inputs(seed: int = 0) -> dict:
    key_of = jax.random.split(jax.random.key(seed), 13)
    table_slab = centred(key_of[0], (ITEMS, D), 1.0, 6.0, ((0, 8),))
    request_rows = with_ends(jax.random.randint(key_of[1], (EVDEV, RQ), 0, ROWS_DEV), jax.random.fold_in(key_of[1], 1), 0, ROWS_DEV - 1).astype(jnp.int32)
    owner_counts = draw_owner_counts(jax.random.fold_in(key_of[12], 71), 0)
    item_slots = draw_item_slots(jax.random.fold_in(key_of[12], 71), 0)
    regroup_counts = draw_regroup_counts(jax.random.fold_in(key_of[12], 71), 0)
    history_lengths = jax.vmap(lambda own: uneven_parts(own, USERS, MB_TOK, LMAX, 1))(jax.random.split(key_of[5], (EVDEV * MICRO))).reshape((EVDEV * MICRO, USERS)).astype(jnp.int32)
    w_proj = centred(key_of[6], (LAYERS, D, PROJ), D ** -0.5, 0.25, ((0, 2),))
    bias_proj = centred(key_of[7], (LAYERS, PROJ), 0.5, 3.0, ((0, 2),), jnp.float32)
    gain_in = jnp.clip(1.0 + 0.1 * jax.random.normal(key_of[8], (LAYERS, D), jnp.float32), 0.5, 1.5)
    gain_mid = jnp.clip(1.0 + 0.1 * jax.random.normal(key_of[9], (LAYERS, D), jnp.float32), 0.5, 1.5)
    rel_bias = centred(key_of[10], (LAYERS, HEADS, LMAX), 1.0, 4.0, ((0, 2),), jnp.float32)
    w_out = centred(key_of[11], (LAYERS, D, D), D ** -0.5, 0.25, ((0, 2),))
    return dict(table_slab=table_slab, request_rows=request_rows, owner_counts=owner_counts, item_slots=item_slots, regroup_counts=regroup_counts, history_lengths=history_lengths, w_proj=w_proj, bias_proj=bias_proj, gain_in=gain_in, gain_mid=gain_mid, rel_bias=rel_bias, w_out=w_out)


def layer_norm(values, gain_row):
    center = values - lax.optimization_barrier(jnp.mean(values, axis=-1, keepdims=True))
    spread = lax.optimization_barrier(jnp.mean(center * center, axis=-1, keepdims=True))
    return center * lax.rsqrt(spread + 1e-05) * gain_row

def user_mask(lengths, row_count):
    limits = jnp.cumsum(lengths).astype(jnp.int32)
    places = jnp.arange(row_count, dtype=jnp.int32)
    owners = lax.optimization_barrier(jnp.sum((places[:, None] >= limits[None, :]).astype(jnp.int32), axis=1))
    return (owners[:, None] == owners[None, :]) & (places[None, :] <= places[:, None])

def bias_grid(rel_table, row_count):
    places = jnp.arange(row_count, dtype=jnp.int32)
    offset = jnp.clip(places[:, None] - places[None, :], 0, rel_table.shape[1] - 1)
    return rel_table[:, offset]

def hstu_block(block_rows, lengths, w_proj, bias_proj, gain_in, gain_mid, grid, w_out):
    row_count, model_width = block_rows.shape
    head_size = model_width // HEADS
    residual = block_rows.astype(jnp.float32)
    normed = layer_norm(residual, gain_in).astype(jnp.bfloat16)
    projected = jnp.dot(normed, w_proj, preferred_element_type=jnp.float32) + bias_proj
    four_parts = jax.nn.silu(projected).astype(jnp.bfloat16)
    gate_part = four_parts[:, :model_width]
    value_part = four_parts[:, model_width:2 * model_width].reshape(row_count, HEADS, head_size)
    query_part = four_parts[:, 2 * model_width:3 * model_width].reshape(row_count, HEADS, head_size)
    key_part = four_parts[:, 3 * model_width:].reshape(row_count, HEADS, head_size)
    scores = jnp.einsum('ihd,jhd->hij', query_part.astype(jnp.float32), key_part.astype(jnp.float32))
    scores = scores * head_size ** (-0.5) + grid
    masked = user_mask(lengths, row_count)[None]
    attend_weights = jnp.where(masked, jax.nn.silu(scores), jnp.zeros_like(scores)).astype(jnp.bfloat16)
    attended = jnp.einsum('hij,jhd->ihd', attend_weights.astype(jnp.float32), value_part.astype(jnp.float32))
    attended = attended.reshape(row_count, model_width)
    gated = (layer_norm(attended, gain_mid) * gate_part.astype(jnp.float32)).astype(jnp.bfloat16)
    return (residual + jnp.dot(gated, w_out, preferred_element_type=jnp.float32)).astype(jnp.bfloat16)

def placed_rows(request_rows, owner_counts, item_slots, regroup_counts):
    limits = jnp.cumsum(owner_counts, axis=1).astype(jnp.int32)
    owners = lax.optimization_barrier(jnp.sum((item_slots[:, :, None] >= limits[:, None, :]).astype(jnp.int32), axis=2))
    listed = jnp.take_along_axis(request_rows, item_slots, axis=1)
    event_rows = (owners * ROWS_DEV + listed).astype(jnp.int32)
    grouped = event_rows.reshape(PEERS, TABLES, TOK_DEV)
    send_plan = regroup_counts
    send_first = jnp.cumsum(send_plan, axis=2).astype(jnp.int32) - send_plan
    recv_last = jnp.cumsum(send_plan, axis=1).astype(jnp.int32)
    recv_first = recv_last - send_plan
    places = jnp.arange(TOK_DEV, dtype=jnp.int32)
    recv_ends = jnp.transpose(recv_last, (0, 2, 1))
    first_by_dest = jnp.transpose(recv_first, (0, 2, 1))
    send_by_dest = jnp.transpose(send_first, (0, 2, 1))
    sources = lax.optimization_barrier(jnp.sum((places[None, None, :, None] >= recv_ends[:, :, None, :]).astype(jnp.int32), axis=3))
    offset = places[None, None, :] - jnp.take_along_axis(first_by_dest, sources, axis=2)
    event_index = jnp.take_along_axis(send_by_dest, sources, axis=2) + offset
    table_index = jnp.arange(TABLES, dtype=jnp.int32)[:, None, None]
    picked = grouped[sources, table_index, event_index]
    return jnp.transpose(picked, (1, 0, 2)).reshape(-1)

def reference(table_slab, request_rows, owner_counts, item_slots, regroup_counts, history_lengths, w_proj, bias_proj, gain_in, gain_mid, rel_bias, w_out):
    row_index = placed_rows(request_rows, owner_counts, item_slots, regroup_counts)
    hidden = table_slab[row_index]
    states = []
    for layer_index in range(LAYERS):
        grid = bias_grid(rel_bias[layer_index], MB_TOK)
        blocks = hidden.reshape(-1, MB_TOK, D)

        def apply_one(block_pair):
            return hstu_block(block_pair[0], block_pair[1], w_proj[layer_index], bias_proj[layer_index], gain_in[layer_index], gain_mid[layer_index], grid, w_out[layer_index])
        hidden = lax.map(apply_one, (blocks, history_lengths)).reshape(-1, D)
        states.append(hidden)
    return jnp.stack(states)
```

```python
import jax
import jax.numpy as jnp
from jax import lax
from jax.sharding import PartitionSpec as P

HEADS = 4
MB_TOK = 256
CAP = 64


def shifted(shard, axis, by):
    peers = lax.axis_size(axis)
    pairs = [(i, i + by) for i in range(peers) if 0 <= i + by < peers]
    return lax.ppermute(shard, axis, pairs)


def running_sum(counts):
    places = jnp.arange(counts.shape[0])
    return jnp.sum(jnp.where(places[None, :] <= places[:, None], counts[None, :], 0), axis=1)


def layer_norm(values, gain_row):
    center = values - jnp.mean(values, axis=-1, keepdims=True)
    spread = jnp.mean(center * center, axis=-1, keepdims=True)
    return center * lax.rsqrt(spread + 1e-05) * gain_row


def user_mask(lengths, row_count):
    limits = running_sum(lengths)
    places = jnp.arange(row_count, dtype=jnp.int32)
    owners = jnp.sum((places[:, None] >= limits[None, :]).astype(jnp.int32), axis=1)
    return (owners[:, None] == owners[None, :]) & (places[None, :] <= places[:, None])


def bias_grid(rel_table, row_count):
    head_count, span = rel_table.shape
    left_fill = jnp.broadcast_to(rel_table[:, :1], (head_count, row_count - 1))
    right_fill = jnp.broadcast_to(rel_table[:, span - 1 :], (head_count, row_count - span))
    widened = jnp.concatenate([left_fill, rel_table, right_fill], axis=1)
    flipped = widened[:, ::-1]
    tiled = jnp.tile(flipped, (1, row_count + 1))
    stride = 2 * row_count - 2
    window = tiled[:, row_count - 1 : row_count - 1 + row_count * stride]
    return window.reshape(head_count, row_count, stride)[:, :, :row_count]


def hstu_block(block_rows, lengths, layer_weights):
    w_proj, bias_proj, gain_in, gain_mid, grid, w_out = layer_weights
    row_count, model_width = block_rows.shape
    head_size = model_width // HEADS
    residual = block_rows.astype(jnp.float32)
    normed = layer_norm(residual, gain_in).astype(jnp.bfloat16)
    projected = jnp.dot(normed, w_proj, preferred_element_type=jnp.float32) + bias_proj
    four_parts = jax.nn.silu(projected).astype(jnp.bfloat16)
    gate_part = four_parts[:, :model_width]
    value_part = four_parts[:, model_width : 2 * model_width].reshape(row_count, HEADS, head_size)
    query_part = four_parts[:, 2 * model_width : 3 * model_width].reshape(
        row_count, HEADS, head_size
    )
    key_part = four_parts[:, 3 * model_width :].reshape(row_count, HEADS, head_size)
    scores = jnp.einsum("ihd,jhd->hij", query_part, key_part, preferred_element_type=jnp.float32)
    scores = scores * head_size ** (-0.5) + grid
    masked = user_mask(lengths, row_count)[None]
    attend_weights = jnp.where(masked, jax.nn.silu(scores), jnp.zeros_like(scores)).astype(
        jnp.bfloat16
    )
    attended = jnp.einsum(
        "hij,jhd->ihd", attend_weights, value_part, preferred_element_type=jnp.float32
    )
    attended = attended.reshape(row_count, model_width)
    gated = (layer_norm(attended, gain_mid) * gate_part.astype(jnp.float32)).astype(jnp.bfloat16)
    return (residual + jnp.dot(gated, w_out, preferred_element_type=jnp.float32)).astype(
        jnp.bfloat16
    )


def fetch_rows(slab_part, request_rows, owner_counts, item_slots):
    row_counts = owner_counts[0]
    owner_total = row_counts.shape[0]
    limits = running_sum(row_counts)
    firsts = limits - row_counts
    offsets = jnp.arange(CAP, dtype=jnp.int32)
    listed = request_rows[0]
    wanted = jnp.minimum(firsts[:, None] + offsets[None, :], listed.shape[0] - 1)
    valid_slot = offsets[None, :] < row_counts[:, None]
    asked_rows = jnp.where(valid_slot, listed[wanted], 0)
    looked_up = slab_part[
        lax.all_to_all(asked_rows, "table", split_axis=0, concat_axis=0, tiled=True)
    ]
    fetched = lax.all_to_all(looked_up, "table", split_axis=0, concat_axis=0, tiled=True)
    slot_list = item_slots[0]
    owner_of = jnp.sum((slot_list[:, None] >= limits[None, :]).astype(jnp.int32), axis=1)
    flat_index = owner_of * CAP + slot_list - firsts[owner_of]
    return fetched.reshape(owner_total * CAP, -1)[flat_index]


def regroup_rows(event_rows, regroup_counts):
    send_plan = regroup_counts[0]
    peer_count = send_plan.shape[0]
    token_count = event_rows.shape[0]
    capacity = token_count // peer_count + token_count // (2 * peer_count)
    seq_index = lax.axis_index("seq")
    sent_counts = send_plan[seq_index]
    send_start = running_sum(sent_counts) - sent_counts
    take_index = jnp.minimum(
        send_start[:, None] + jnp.arange(capacity, dtype=jnp.int32)[None, :], token_count - 1
    )
    outgoing = event_rows[take_index]
    incoming = lax.all_to_all(outgoing, "seq", split_axis=0, concat_axis=0, tiled=True)
    got_counts = send_plan[:, seq_index]
    recv_last = running_sum(got_counts)
    recv_first = recv_last - got_counts
    places = jnp.arange(token_count, dtype=jnp.int32)
    sources = jnp.sum((places[:, None] >= recv_last[None, :]).astype(jnp.int32), axis=1)
    pick_index = sources * capacity + places - recv_first[sources]
    return incoming.reshape(peer_count * capacity, -1)[pick_index]


def shards(
    table_slab,
    request_rows,
    owner_counts,
    item_slots,
    regroup_counts,
    history_lengths,
    w_proj,
    bias_proj,
    gain_in,
    gain_mid,
    rel_bias,
    w_out,
):
    full_width = table_slab.shape[1]
    section_index = lax.axis_index("section")
    first_section = section_index == 0
    events = regroup_rows(
        fetch_rows(table_slab, request_rows, owner_counts, item_slots), regroup_counts
    )
    micro_count = events.shape[0] // MB_TOK
    blocks = events.reshape(micro_count, MB_TOK, full_width)
    layer_weights = (
        w_proj[0],
        bias_proj[0],
        gain_in[0],
        gain_mid[0],
        bias_grid(rel_bias[0], MB_TOK),
        w_out[0],
    )
    outputs = []
    carried = blocks[0]
    for moment in range(micro_count + 1):
        front_pick = min(moment, micro_count - 1)
        back_pick = max(moment - 1, 0)
        if moment == 0:
            source_rows = blocks[0]
        else:
            received = shifted(carried, "section", 1)
            source_rows = jnp.where(first_section, blocks[front_pick], received)
        lengths_now = jnp.where(
            first_section, history_lengths[front_pick], history_lengths[back_pick]
        )
        carried = hstu_block(source_rows, lengths_now, layer_weights)
        outputs.append(carried)
    result = jnp.where(first_section, jnp.stack(outputs[:micro_count]), jnp.stack(outputs[1:]))
    return result.reshape(1, micro_count * MB_TOK, full_width)


def solution(mesh):
    in_specs = (
        P("table", None),
        P(("seq", "table"), None),
        P(("seq", "table"), None),
        P(("seq", "table"), None),
        P("table", None, None),
        P(("seq", "table"), None),
        P("section", None, None),
        P("section", None),
        P("section", None),
        P("section", None),
        P("section", None, None),
        P("section", None, None),
    )
    out_specs = P("section", ("seq", "table"), None)
    return jax.shard_map(shards, mesh=mesh, in_specs=in_specs, out_specs=out_specs, check_vma=False)
```

```python
import functools

import jax
import jax.numpy as jnp
from jax import lax
from jax.experimental import pallas as pl
from jax.experimental.pallas import tpu as pltpu
from jax.sharding import PartitionSpec as P

HEADS = 4
MB_TOK = 256
CAP = 64
LANES = 128
MESH = pl.DeviceIdType.MESH
F32 = jnp.float32
BF16 = jnp.bfloat16


def iota(shape, axis):
    return lax.broadcasted_iota(jnp.int32, shape, axis)


def normalise(values):
    center = values - jnp.mean(values, axis=-1, keepdims=True)
    spread = jnp.mean(center * center, axis=-1, keepdims=True)
    return center * lax.rsqrt(spread + 1e-05)


def silu_of_half(half):
    return half + half * jnp.tanh(half)


def kernel(
    dims,
    slab_hbm,
    req_ref,
    counts_smem,
    slots_ref,
    plan_smem,
    lengths_smem,
    wp_hbm,
    bias_ref,
    gin_ref,
    gmid_ref,
    rel_ref,
    wo_hbm,
    out_ref,
    slab,
    wp,
    wo,
    par,
    msg,
    flat,
    ids,
    gath,
    rows,
    grid,
    mask,
    made,
    local_sem,
    wsend,
    wrecv,
    msend,
    mrecv,
    fsend,
    frecv,
    rsend,
    rrecv,
    xsend,
    xrecv,
    ssend,
    srecv,
    osend,
    orecv,
):
    peers, tables = dims
    half = CAP // 2
    width = slab.shape[1]
    span = LANES
    tokens = slots_ref.shape[1]
    mine = tokens // 2
    micro = mine // MB_TOK
    listed = req_ref.shape[1] // LANES
    slab_rows = slab.shape[0]
    block_rows = 2 * tables * half
    users = lengths_smem.shape[1]
    head_size = width // HEADS
    c = lax.axis_index("section")
    s = lax.axis_index("seq")
    t = lax.axis_index("table")
    sib = (1 - c, s, t)

    def table_peer(k):
        return lax.rem(t + k, tables)

    def seq_peer(k):
        return lax.rem(s + k, peers)

    def remote(src, dst, send, recv, to):
        return pltpu.make_async_remote_copy(
            src_ref=src,
            dst_ref=dst,
            send_sem=send,
            recv_sem=recv,
            device_id=to,
            device_id_type=MESH,
        )

    slab_copy = pltpu.make_async_copy(slab_hbm, slab, local_sem.at[0])
    wp_copy = pltpu.make_async_copy(wp_hbm.at[0], wp.at[c], local_sem.at[1])
    wo_copy = pltpu.make_async_copy(wo_hbm.at[0], wo.at[c], local_sem.at[2])
    slab_copy.start()
    wp_copy.start()
    wo_copy.start()

    barrier = pltpu.get_barrier_semaphore()

    def greet_table(k, carry):
        pl.semaphore_signal(barrier, inc=1, device_id=(c, s, table_peer(k)), device_id_type=MESH)
        return carry

    def greet_seq(k, carry):
        pl.semaphore_signal(barrier, inc=1, device_id=(c, seq_peer(k), t), device_id_type=MESH)
        return carry

    lax.fori_loop(1, tables, greet_table, 0)
    lax.fori_loop(1, peers, greet_seq, 0)
    pl.semaphore_signal(barrier, inc=1, device_id=sib, device_id_type=MESH)

    for k in range(listed):
        msg[t, k : k + 1, :] = req_ref[0:1, k * LANES : (k + 1) * LANES]
    lane = iota((1, LANES), 1)
    first_row = jnp.zeros((1, LANES), jnp.int32)
    limit = jnp.int32(0)
    limits = []
    for o in range(tables):
        first_row = jnp.where(lane == o, limit, first_row)
        limit = limit + counts_smem[0, o]
        limits.append(limit)
    msg[t, listed : listed + 1, :] = first_row

    for k in range(tokens // LANES):
        slot = slots_ref[0:1, k * LANES : (k + 1) * LANES]
        owner = jnp.zeros((1, LANES), jnp.int32)
        first = jnp.zeros((1, LANES), jnp.int32)
        for o in range(tables):
            past = slot >= limits[o]
            owner = owner + jnp.where(past, 1, 0)
            first = jnp.where(past, limits[o], first)
        place = slot - first
        place = place + owner * half + jnp.where(place >= half, (tables - 1) * half, 0)
        flat[s, k : k + 1, :] = place

    for k in range(4):
        par[c, k : k + 1, :] = bias_ref[0:1, k * width : (k + 1) * width] * 0.5
    par[c, 4:5, :] = gin_ref[...]
    par[c, 5:6, :] = gmid_ref[...]
    for k in range(HEADS):
        par[c, 8 + k : 9 + k, 0:span] = rel_ref[0, k : k + 1, :] * 0.5

    pl.semaphore_wait(barrier, (tables - 1) + (peers - 1) + 1)

    def ask(k):
        return remote(msg.at[t], msg.at[t], msend.at[k], mrecv.at[t], (c, s, table_peer(k)))

    def ask_step(k, carry):
        ask(k).start()
        return carry

    lax.fori_loop(1, tables, ask_step, 0)

    def tell(k):
        return remote(flat.at[s], flat.at[s], fsend.at[k], frecv.at[s], (c, seq_peer(k), t))

    def tell_step(k, carry):
        tell(k).start()
        return carry

    lax.fori_loop(1, peers, tell_step, 0)
    par_copy = remote(par.at[c], par.at[c], wsend.at[0], wrecv.at[0], sib)
    wp_send = remote(wp_hbm.at[0], wp.at[c], wsend.at[1], wrecv.at[1], sib)
    wo_send = remote(wo_hbm.at[0], wo.at[c], wsend.at[2], wrecv.at[2], sib)
    par_copy.start()
    wp_send.start()
    wo_send.start()

    lower = MB_TOK // 2
    for m in range(micro):
        row_owner = jnp.zeros((1, MB_TOK), jnp.int32)
        col_owner = jnp.zeros((MB_TOK, 1), jnp.int32)
        place_row = iota((1, MB_TOK), 1)
        place_col = iota((MB_TOK, 1), 0)
        end = jnp.int32(0)
        for u in range(users):
            end = end + lengths_smem[c * micro + m, u]
            row_owner = row_owner + jnp.where(place_row >= end, 1, 0)
            col_owner = col_owner + jnp.where(place_col >= end, 1, 0)
        top = (col_owner[:lower] == row_owner[:, :lower]) & (place_row[:, :lower] <= place_col[:lower])
        low = (col_owner[lower:] == row_owner) & (place_row <= place_col[lower:])
        mask[m, :, 0:lower] = jnp.where(top, 1.0, 0.0)
        mask[m, :, lower:] = jnp.where(low, 1.0, 0.0)

    def hear(k, carry):
        o = table_peer(k)
        remote(msg.at[o], msg.at[o], msend.at[k], mrecv.at[o], (c, s, o)).wait_recv()
        return carry

    lax.fori_loop(1, tables, hear, 0)

    def read_ids(o, carry):
        firsts = msg[o, listed : listed + 1, :]
        first = jnp.sum(jnp.where(lane == t, firsts, 0).astype(F32), axis=1, keepdims=True)
        want = first.astype(jnp.int32) + c * half + iota((half, LANES), 0)
        total = jnp.zeros((half, LANES), F32)
        for k in range(listed):
            listed_row = msg[o, k : k + 1, :].astype(F32)
            total = total + jnp.where(iota((half, LANES), 1) + k * LANES == want, listed_row, 0.0)
        found = jnp.sum(total, axis=1, keepdims=True).astype(jnp.int32)
        ids[o] = jnp.broadcast_to(found, (half, LANES))
        return carry

    lax.fori_loop(0, tables, read_ids, 0)
    slab_copy.wait()
    wanted = ids[...].reshape(tables * half, LANES)
    spots = iota((tables * half, LANES), 1)
    picks = jnp.concatenate(
        [jnp.where(wanted == spots + k * LANES, 1.0, 0.0).astype(BF16) for k in range(slab_rows // LANES)],
        axis=1,
    )
    looked_up = jnp.dot(picks, slab[...], preferred_element_type=F32).astype(BF16)
    gath[...] = looked_up.reshape(tables, half, width)

    def serve(k):
        o = table_peer(k)
        return remote(gath.at[o], rows.at[s, c, t], rsend.at[k], rrecv.at[t], (c, s, o))

    def serve_step(k, carry):
        serve(k).start()
        return carry

    lax.fori_loop(1, tables, serve_step, 0)
    rows[s, c, t] = gath[t]

    def across(k, o):
        place = rows.at[s, c, o]
        return remote(place, place, xsend.at[k, o], xrecv.at[s, o], (c, seq_peer(k), t))

    def beside(source, o):
        place = rows.at[source, c, o]
        return remote(place, place, ssend.at[source, o], srecv.at[source, o], sib)

    def pass_on(o):
        def one(k, carry):
            across(k, o).start()
            return carry

        lax.fori_loop(1, peers, one, 0)
        beside(s, o).start()

    pass_on(t)

    wp_copy.wait()
    wo_copy.wait()
    par_copy.wait_recv()
    for layer in range(2):
        for head in range(HEADS):
            rel_row = jnp.broadcast_to(par[layer, 8 + head : 9 + head, 0:span], (span, span))
            rel_col = jnp.sum(
                jnp.where(iota((span, span), 0) == iota((span, span), 1), rel_row, 0.0), axis=1, keepdims=True
            )
            turned = jnp.where(
                iota((span, 2 * span), 0) + iota((span, 2 * span), 1) == span, rel_col, 0.0
            )
            base = jnp.broadcast_to(jnp.sum(turned, axis=0, keepdims=True), (span, 2 * span))
            grid[layer, head] = pltpu.roll(base, 0, 1, stride=1, stride_axis=0)

    def heard(k, carry):
        source = seq_peer(k)
        remote(flat.at[source], flat.at[source], fsend.at[k], frecv.at[source], (c, source, t)).wait_recv()
        return carry

    lax.fori_loop(1, peers, heard, 0)

    def collect(k, carry):
        o = table_peer(k)
        remote(gath.at[o], rows.at[s, c, o], rsend.at[k], rrecv.at[o], (c, s, o)).wait_recv()
        pass_on(o)
        return carry

    lax.fori_loop(1, tables, collect, 0)

    def second(i, carry):
        source = seq_peer(1 + i // tables)
        o = table_peer(lax.rem(i, tables))
        place = rows.at[source, c, o]
        remote(place, place, xsend.at[1, o], xrecv.at[source, o], (c, source, t)).wait_recv()
        beside(source, o).start()
        return carry

    chunk = mine
    places = iota((chunk, LANES), 0) + c * mine
    total = jnp.zeros((chunk, LANES), F32)
    for source in range(peers):
        sent_first = jnp.int32(0)
        got_first = jnp.int32(0)
        for other in range(peers):
            sent_first = sent_first + jnp.where(other < s, plan_smem[0, source, other], 0)
            if other < source:
                got_first = got_first + plan_smem[0, other, s]
        number = plan_smem[0, source, s]
        for k in range(tokens // LANES):
            rank = lane + k * LANES - sent_first
            inside = (rank >= 0) & (rank < number)
            position = jnp.where(inside, rank + got_first, -1)
            value = (flat[source, k : k + 1, :] + source * block_rows).astype(F32)
            total = total + jnp.where(places == position, value, 0.0)
    index = jnp.sum(total, axis=1, keepdims=True).astype(jnp.int32)

    lax.fori_loop(0, (peers - 1) * tables, second, 0)

    def arrived(i, carry):
        source = i // tables
        o = lax.rem(i, tables)
        place = rows.at[source, 1 - c, o]
        remote(place, place, ssend.at[source, o], srecv.at[source, o], sib).wait_recv()
        return carry

    lax.fori_loop(0, peers * tables, arrived, 0)

    hidden = jnp.zeros((mine, width), F32)
    for source in range(peers):
        picks = jnp.where(index == iota((1, block_rows), 1) + source * block_rows, 1.0, 0.0).astype(BF16)
        hidden = hidden + jnp.dot(
            picks, rows[source].reshape(block_rows, width), preferred_element_type=F32
        )

    wp_send.wait_recv()
    wo_send.wait_recv()

    out_copy = remote(
        made.at[1 - c], out_ref.at[0, pl.ds(c * mine, mine)], osend.at[0], orecv.at[0], sib
    )
    for layer in range(2):
        normed = (normalise(hidden) * par[layer, 4:5, :]).astype(BF16)
        parts = []
        for k in range(4):
            projected = jnp.dot(
                normed, wp[layer, :, k * width : (k + 1) * width], preferred_element_type=F32
            )
            parts.append(silu_of_half(projected * 0.5 + par[layer, k : k + 1, :]).astype(BF16))
        gate, value, query, key = parts
        scale = 0.5 * head_size ** (-0.5)
        contract = (((1,), (1,)), ((), ()))
        batches = []
        for m in range(micro):
            r0, r1, r2 = m * MB_TOK, m * MB_TOK + lower, (m + 1) * MB_TOK
            heads = []
            for head in range(HEADS):
                f0, f1 = head * head_size, (head + 1) * head_size
                k_all = key[r0:r2, f0:f1]
                v_all = value[r0:r2, f0:f1]
                top = lax.dot_general(
                    query[r0:r1, f0:f1], k_all[:lower], contract, preferred_element_type=F32
                )
                low = lax.dot_general(query[r1:r2, f0:f1], k_all, contract, preferred_element_type=F32)
                top = silu_of_half(top * scale + grid[layer, head, :, lower:])
                low = silu_of_half(low * scale + grid[layer, head])
                top = (top * mask[m, :, 0:lower]).astype(BF16)
                low = (low * mask[m, :, lower:]).astype(BF16)
                heads.append(
                    jnp.concatenate(
                        [
                            jnp.dot(top, v_all[:lower], preferred_element_type=F32),
                            jnp.dot(low, v_all, preferred_element_type=F32),
                        ],
                        axis=0,
                    )
                )
            batches.append(jnp.concatenate(heads, axis=1))
        attended = jnp.concatenate(batches, axis=0)
        gated = (normalise(attended) * par[layer, 5:6, :] * gate.astype(F32)).astype(BF16)
        state = (hidden + jnp.dot(gated, wo[layer], preferred_element_type=F32)).astype(BF16)
        hidden = state.astype(F32)

        @pl.when(c == layer)
        def _():
            out_ref[0, pl.ds(pl.multiple_of(c * mine, mine), mine), :] = state

        @pl.when(c != layer)
        def _():
            made[layer] = state
            out_copy.start()

    def sent_table(k, carry):
        ask(k).wait_send()
        serve(k).wait_send()
        return carry

    def sent_seq(k, carry):
        tell(k).wait_send()
        return carry

    def sent_across(i, carry):
        across(1 + i // tables, lax.rem(i, tables)).wait_send()
        return carry

    def sent_beside(i, carry):
        beside(i // tables, lax.rem(i, tables)).wait_send()
        return carry

    lax.fori_loop(1, tables, sent_table, 0)
    lax.fori_loop(1, peers, sent_seq, 0)
    lax.fori_loop(0, (peers - 1) * tables, sent_across, 0)
    lax.fori_loop(0, peers * tables, sent_beside, 0)
    par_copy.wait_send()
    wp_send.wait_send()
    wo_send.wait_send()
    out_copy.wait()


def shards(
    table_slab,
    request_rows,
    owner_counts,
    item_slots,
    regroup_counts,
    history_lengths,
    w_proj,
    bias_proj,
    gain_in,
    gain_mid,
    rel_bias,
    w_out,
):
    peers = lax.axis_size("seq")
    tables = lax.axis_size("table")
    slab_rows, width = table_slab.shape
    tokens = item_slots.shape[1]
    half = CAP // 2
    msg_rows = (request_rows.shape[1] // LANES + 1 + 7) // 8 * 8
    micro = tokens // 2 // MB_TOK
    vmem = pl.BlockSpec(memory_space=pltpu.VMEM)
    smem = pl.BlockSpec(memory_space=pltpu.SMEM)
    hbm = pl.BlockSpec(memory_space=pl.ANY)
    dma = pltpu.SemaphoreType.DMA
    return pl.pallas_call(
        functools.partial(kernel, (peers, tables)),
        out_shape=jax.ShapeDtypeStruct((1, tokens, width), BF16),
        in_specs=[hbm, vmem, smem, vmem, smem, smem, hbm, vmem, vmem, vmem, vmem, hbm],
        out_specs=vmem,
        scratch_shapes=[
            pltpu.VMEM((slab_rows, width), BF16),
            pltpu.VMEM((2, width, 4 * width), BF16),
            pltpu.VMEM((2, width, width), BF16),
            pltpu.VMEM((2, 16, width), F32),
            pltpu.VMEM((tables, msg_rows, LANES), jnp.int32),
            pltpu.VMEM((peers, tokens // LANES, LANES), jnp.int32),
            pltpu.VMEM((tables, half, LANES), jnp.int32),
            pltpu.VMEM((tables, half, width), BF16),
            pltpu.VMEM((peers, 2, tables, half, width), BF16),
            pltpu.VMEM((2, HEADS, LANES, 2 * LANES), F32),
            pltpu.VMEM((micro, MB_TOK // 2, MB_TOK + MB_TOK // 2), F32),
            pltpu.VMEM((2, tokens // 2, width), BF16),
            dma((3,)),
            dma((3,)),
            dma((3,)),
            dma((tables,)),
            dma((tables,)),
            dma((peers,)),
            dma((peers,)),
            dma((tables,)),
            dma((tables,)),
            dma((peers, tables)),
            dma((peers, tables)),
            dma((peers, tables)),
            dma((peers, tables)),
            dma((1,)),
            dma((1,)),
        ],
        compiler_params=pltpu.CompilerParams(
            collective_id=0, has_side_effects=True, vmem_limit_bytes=48 * 1024 * 1024
        ),
        name="hstu_window",
    )(
        table_slab,
        request_rows,
        owner_counts,
        item_slots,
        regroup_counts,
        history_lengths,
        w_proj,
        bias_proj,
        gain_in,
        gain_mid,
        rel_bias,
        w_out,
    )


def solution(mesh):
    in_specs = (
        P("table", None),
        P(("seq", "table"), None),
        P(("seq", "table"), None),
        P(("seq", "table"), None),
        P("table", None, None),
        P(("seq", "table"), None),
        P("section", None, None),
        P("section", None),
        P("section", None),
        P("section", None),
        P("section", None, None),
        P("section", None, None),
    )
    out_specs = P("section", ("seq", "table"), None)
    return jax.shard_map(shards, mesh=mesh, in_specs=in_specs, out_specs=out_specs, check_vma=False)
```

```python
import functools

import jax
import jax.numpy as jnp
from jax import lax
from jax.experimental import pallas as pl
from jax.experimental.pallas import tpu as pltpu
from jax.sharding import PartitionSpec as P

HEADS = 4
MB_TOK = 256
CAP = 64
LANES = 128
MESH = pl.DeviceIdType.MESH
F32 = jnp.float32
BF16 = jnp.bfloat16


def iota(shape, axis):
    return lax.broadcasted_iota(jnp.int32, shape, axis)


def normalise(values):
    center = values - jnp.mean(values, axis=-1, keepdims=True)
    spread = jnp.mean(center * center, axis=-1, keepdims=True)
    return center * lax.rsqrt(spread + 1e-05)


def silu_of_half(half):
    return half + half * jnp.tanh(half)


def kernel(
    dims,
    slab_hbm,
    req_hbm,
    counts_hbm,
    slots_hbm,
    plan_hbm,
    lengths_hbm,
    wp_hbm,
    bias_hbm,
    gin_hbm,
    gmid_hbm,
    rel_hbm,
    wo_hbm,
    out_ref,
    req_ref,
    counts_smem,
    slots_ref,
    plan_smem,
    lengths_smem,
    bias_ref,
    gin_ref,
    gmid_ref,
    rel_ref,
    slab,
    wp,
    wo,
    par,
    msg,
    flat,
    ids,
    gath,
    rows,
    grid,
    mask,
    made,
    local_sem,
    wsend,
    wrecv,
    msend,
    mrecv,
    fsend,
    frecv,
    rsend,
    rrecv,
    xsend,
    xrecv,
    ssend,
    srecv,
    osend,
    orecv,
):
    peers, tables = dims
    half = CAP // 2
    width = slab.shape[1]
    span = LANES
    tokens = slots_ref.shape[1]
    mine = tokens // 2
    micro = mine // MB_TOK
    listed = req_ref.shape[1] // LANES
    slab_rows = slab.shape[0]
    block_rows = 2 * tables * half
    users = lengths_smem.shape[1]
    head_size = width // HEADS
    c = lax.axis_index("section")
    s = lax.axis_index("seq")
    t = lax.axis_index("table")
    sib = (1 - c, s, t)

    def table_peer(k):
        if tables & (tables - 1):
            return lax.rem(t + k, tables)
        flipped = 0
        bit = 1
        while bit < tables:
            own = lax.rem(t // bit, 2)
            turn = lax.rem(k // bit, 2)
            flipped = flipped + bit * (own + turn - 2 * own * turn)
            bit = 2 * bit
        return flipped

    def seq_peer(k):
        return lax.rem(s + k, peers)

    def remote(src, dst, send, recv, to):
        return pltpu.make_async_remote_copy(
            src_ref=src,
            dst_ref=dst,
            send_sem=send,
            recv_sem=recv,
            device_id=to,
            device_id_type=MESH,
        )

    small = [
        pltpu.make_async_copy(source, place, local_sem.at[3 + k])
        for k, (source, place) in enumerate(
            (
                (counts_hbm, counts_smem),
                (req_hbm, req_ref),
                (slots_hbm, slots_ref),
                (bias_hbm, bias_ref),
                (gin_hbm, gin_ref),
                (gmid_hbm, gmid_ref),
                (rel_hbm, rel_ref),
                (lengths_hbm, lengths_smem),
                (plan_hbm, plan_smem),
            )
        )
    ]
    for copy in small:
        copy.start()
    slab_copy = pltpu.make_async_copy(slab_hbm, slab, local_sem.at[0])
    wp_copy = pltpu.make_async_copy(wp_hbm.at[0], wp.at[c], local_sem.at[1])
    wo_copy = pltpu.make_async_copy(wo_hbm.at[0], wo.at[c], local_sem.at[2])
    slab_copy.start()
    wp_copy.start()
    wo_copy.start()

    barrier = pltpu.get_barrier_semaphore()

    def greet_table(k, carry):
        pl.semaphore_signal(barrier, inc=1, device_id=(c, s, table_peer(k)), device_id_type=MESH)
        return carry

    def greet_seq(k, carry):
        pl.semaphore_signal(barrier, inc=1, device_id=(c, seq_peer(k), t), device_id_type=MESH)
        return carry

    lax.fori_loop(1, tables, greet_table, 0)
    lax.fori_loop(1, peers, greet_seq, 0)
    pl.semaphore_signal(barrier, inc=1, device_id=sib, device_id_type=MESH)

    for copy in small:
        copy.wait()

    for k in range(listed):
        msg[t, k : k + 1, :] = req_ref[0:1, k * LANES : (k + 1) * LANES]
    lane = iota((1, LANES), 1)
    first_row = jnp.zeros((1, LANES), jnp.int32)
    limit = jnp.int32(0)
    limits = []
    for o in range(tables):
        first_row = jnp.where(lane == o, limit, first_row)
        limit = limit + counts_smem[0, o]
        limits.append(limit)
    msg[t, listed : listed + 1, :] = first_row

    for k in range(tokens // LANES):
        slot = slots_ref[0:1, k * LANES : (k + 1) * LANES]
        owner = jnp.zeros((1, LANES), jnp.int32)
        first = jnp.zeros((1, LANES), jnp.int32)
        for o in range(tables):
            past = slot >= limits[o]
            owner = owner + jnp.where(past, 1, 0)
            first = jnp.where(past, limits[o], first)
        place = slot - first
        place = place + owner * half + jnp.where(place >= half, (tables - 1) * half, 0)
        flat[s, k : k + 1, :] = place

    for k in range(4):
        par[c, k : k + 1, :] = bias_ref[0:1, k * width : (k + 1) * width] * 0.5
    par[c, 4:5, :] = gin_ref[...]
    par[c, 5:6, :] = gmid_ref[...]
    for k in range(HEADS):
        par[c, 8 + k : 9 + k, 0:span] = rel_ref[0, k : k + 1, :] * 0.5

    pl.semaphore_wait(barrier, (tables - 1) + (peers - 1) + 1)

    def ask(k):
        return remote(msg.at[t], msg.at[t], msend.at[k], mrecv.at[t], (c, s, table_peer(k)))

    def ask_step(k, carry):
        ask(k).start()
        return carry

    lax.fori_loop(1, tables, ask_step, 0)

    def tell(k):
        return remote(flat.at[s], flat.at[s], fsend.at[k], frecv.at[s], (c, seq_peer(k), t))

    def tell_step(k, carry):
        tell(k).start()
        return carry

    lax.fori_loop(1, peers, tell_step, 0)
    par_copy = remote(par.at[c], par.at[c], wsend.at[0], wrecv.at[0], sib)
    wp_send = remote(wp_hbm.at[0], wp.at[c], wsend.at[1], wrecv.at[1], sib)
    wo_send = remote(wo_hbm.at[0], wo.at[c], wsend.at[2], wrecv.at[2], sib)
    par_copy.start()
    wp_send.start()
    wo_send.start()

    lower = MB_TOK // 2
    for m in range(micro):
        row_owner = jnp.zeros((1, MB_TOK), jnp.int32)
        col_owner = jnp.zeros((MB_TOK, 1), jnp.int32)
        place_row = iota((1, MB_TOK), 1)
        place_col = iota((MB_TOK, 1), 0)
        end = jnp.int32(0)
        for u in range(users):
            end = end + lengths_smem[c * micro + m, u]
            row_owner = row_owner + jnp.where(place_row >= end, 1, 0)
            col_owner = col_owner + jnp.where(place_col >= end, 1, 0)
        top = (col_owner[:lower] == row_owner[:, :lower]) & (place_row[:, :lower] <= place_col[:lower])
        low = (col_owner[lower:] == row_owner) & (place_row <= place_col[lower:])
        mask[m, :, 0:lower] = jnp.where(top, 1.0, 0.0)
        mask[m, :, lower:] = jnp.where(low, 1.0, 0.0)

    def hear(k, carry):
        o = table_peer(k)
        remote(msg.at[o], msg.at[o], msend.at[k], mrecv.at[o], (c, s, o)).wait_recv()
        return carry

    lax.fori_loop(1, tables, hear, 0)

    def read_ids(o, carry):
        firsts = msg[o, listed : listed + 1, :]
        first = jnp.sum(jnp.where(lane == t, firsts, 0).astype(F32), axis=1, keepdims=True)
        want = first.astype(jnp.int32) + c * half + iota((half, LANES), 0)
        total = jnp.zeros((half, LANES), F32)
        for k in range(listed):
            listed_row = msg[o, k : k + 1, :].astype(F32)
            total = total + jnp.where(iota((half, LANES), 1) + k * LANES == want, listed_row, 0.0)
        found = jnp.sum(total, axis=1, keepdims=True).astype(jnp.int32)
        ids[o] = jnp.broadcast_to(found, (half, LANES))
        return carry

    lax.fori_loop(0, tables, read_ids, 0)
    slab_copy.wait()
    wanted = ids[...].reshape(tables * half, LANES)
    spots = iota((tables * half, LANES), 1)
    picks = jnp.concatenate(
        [jnp.where(wanted == spots + k * LANES, 1.0, 0.0).astype(BF16) for k in range(slab_rows // LANES)],
        axis=1,
    )
    looked_up = jnp.dot(picks, slab[...], preferred_element_type=F32).astype(BF16)
    gath[...] = looked_up.reshape(tables, half, width)

    def serve(k):
        o = table_peer(k)
        return remote(gath.at[o], rows.at[s, c, t], rsend.at[k], rrecv.at[t], (c, s, o))

    def serve_step(k, carry):
        serve(k).start()
        return carry

    lax.fori_loop(1, tables, serve_step, 0)
    rows[s, c, t] = gath[t]

    def across(k, o):
        place = rows.at[s, c, o]
        return remote(place, place, xsend.at[k, o], xrecv.at[s, o], (c, seq_peer(k), t))

    def beside(source, o):
        place = rows.at[source, c, o]
        return remote(place, place, ssend.at[source, o], srecv.at[source, o], sib)

    def pass_on(o):
        def one(k, carry):
            across(k, o).start()
            return carry

        lax.fori_loop(1, peers, one, 0)
        beside(s, o).start()

    pass_on(t)

    wp_copy.wait()
    wo_copy.wait()
    par_copy.wait_recv()
    for layer in range(2):
        for head in range(HEADS):
            rel_row = jnp.broadcast_to(par[layer, 8 + head : 9 + head, 0:span], (span, span))
            rel_col = jnp.sum(
                jnp.where(iota((span, span), 0) == iota((span, span), 1), rel_row, 0.0), axis=1, keepdims=True
            )
            turned = jnp.where(
                iota((span, 2 * span), 0) + iota((span, 2 * span), 1) == span, rel_col, 0.0
            )
            base = jnp.broadcast_to(jnp.sum(turned, axis=0, keepdims=True), (span, 2 * span))
            grid[layer, head] = pltpu.roll(base, 0, 1, stride=1, stride_axis=0)

    def heard(k, carry):
        source = seq_peer(k)
        remote(flat.at[source], flat.at[source], fsend.at[k], frecv.at[source], (c, source, t)).wait_recv()
        return carry

    lax.fori_loop(1, peers, heard, 0)

    def collect(k, carry):
        o = table_peer(k)
        remote(gath.at[o], rows.at[s, c, o], rsend.at[k], rrecv.at[o], (c, s, o)).wait_recv()
        pass_on(o)
        return carry

    lax.fori_loop(1, tables, collect, 0)

    def second(i, carry):
        source = seq_peer(1 + i // tables)
        o = table_peer(lax.rem(i, tables))
        place = rows.at[source, c, o]
        remote(place, place, xsend.at[1, o], xrecv.at[source, o], (c, source, t)).wait_recv()
        beside(source, o).start()
        return carry

    chunk = mine
    places = iota((chunk, LANES), 0) + c * mine
    total = jnp.zeros((chunk, LANES), F32)
    for source in range(peers):
        sent_first = jnp.int32(0)
        got_first = jnp.int32(0)
        for other in range(peers):
            sent_first = sent_first + jnp.where(other < s, plan_smem[0, source, other], 0)
            if other < source:
                got_first = got_first + plan_smem[0, other, s]
        number = plan_smem[0, source, s]
        for k in range(tokens // LANES):
            rank = lane + k * LANES - sent_first
            inside = (rank >= 0) & (rank < number)
            position = jnp.where(inside, rank + got_first, -1)
            value = (flat[source, k : k + 1, :] + source * block_rows).astype(F32)
            total = total + jnp.where(places == position, value, 0.0)
    index = jnp.sum(total, axis=1, keepdims=True).astype(jnp.int32)

    lax.fori_loop(0, (peers - 1) * tables, second, 0)

    def arrived(i, carry):
        source = i // tables
        o = lax.rem(i, tables)
        place = rows.at[source, 1 - c, o]
        remote(place, place, ssend.at[source, o], srecv.at[source, o], sib).wait_recv()
        return carry

    lax.fori_loop(0, peers * tables, arrived, 0)

    hidden = jnp.zeros((mine, width), F32)
    for source in range(peers):
        picks = jnp.where(index == iota((1, block_rows), 1) + source * block_rows, 1.0, 0.0).astype(BF16)
        hidden = hidden + jnp.dot(
            picks, rows[source].reshape(block_rows, width), preferred_element_type=F32
        )

    wp_send.wait_recv()
    wo_send.wait_recv()

    out_copy = remote(
        made.at[1 - c], out_ref.at[0, pl.ds(c * mine, mine)], osend.at[0], orecv.at[0], sib
    )
    own_copy = pltpu.make_async_copy(
        made.at[c], out_ref.at[0, pl.ds(c * mine, mine)], local_sem.at[12]
    )
    for layer in range(2):
        normed = (normalise(hidden) * par[layer, 4:5, :]).astype(BF16)
        parts = []
        for k in range(4):
            projected = jnp.dot(
                normed, wp[layer, :, k * width : (k + 1) * width], preferred_element_type=F32
            )
            parts.append(silu_of_half(projected * 0.5 + par[layer, k : k + 1, :]).astype(BF16))
        gate, value, query, key = parts
        scale = 0.5 * head_size ** (-0.5)
        contract = (((1,), (1,)), ((), ()))
        batches = []
        for m in range(micro):
            r0, r1, r2 = m * MB_TOK, m * MB_TOK + lower, (m + 1) * MB_TOK
            heads = []
            for head in range(HEADS):
                f0, f1 = head * head_size, (head + 1) * head_size
                k_all = key[r0:r2, f0:f1]
                v_all = value[r0:r2, f0:f1]
                top = lax.dot_general(
                    query[r0:r1, f0:f1], k_all[:lower], contract, preferred_element_type=F32
                )
                low = lax.dot_general(query[r1:r2, f0:f1], k_all, contract, preferred_element_type=F32)
                top = silu_of_half(top * scale + grid[layer, head, :, lower:])
                low = silu_of_half(low * scale + grid[layer, head])
                top = (top * mask[m, :, 0:lower]).astype(BF16)
                low = (low * mask[m, :, lower:]).astype(BF16)
                heads.append(
                    jnp.concatenate(
                        [
                            jnp.dot(top, v_all[:lower], preferred_element_type=F32),
                            jnp.dot(low, v_all, preferred_element_type=F32),
                        ],
                        axis=0,
                    )
                )
            batches.append(jnp.concatenate(heads, axis=1))
        attended = jnp.concatenate(batches, axis=0)
        gated = (normalise(attended) * par[layer, 5:6, :] * gate.astype(F32)).astype(BF16)
        state = (hidden + jnp.dot(gated, wo[layer], preferred_element_type=F32)).astype(BF16)
        hidden = state.astype(F32)

        made[layer] = state

        @pl.when(c == layer)
        def _():
            own_copy.start()

        @pl.when(c != layer)
        def _():
            out_copy.start()

    def sent_table(k, carry):
        ask(k).wait_send()
        serve(k).wait_send()
        return carry

    def sent_seq(k, carry):
        tell(k).wait_send()
        return carry

    def sent_across(i, carry):
        across(1 + i // tables, lax.rem(i, tables)).wait_send()
        return carry

    def sent_beside(i, carry):
        beside(i // tables, lax.rem(i, tables)).wait_send()
        return carry

    lax.fori_loop(1, tables, sent_table, 0)
    lax.fori_loop(1, peers, sent_seq, 0)
    lax.fori_loop(0, (peers - 1) * tables, sent_across, 0)
    lax.fori_loop(0, peers * tables, sent_beside, 0)
    par_copy.wait_send()
    wp_send.wait_send()
    wo_send.wait_send()
    own_copy.wait()
    out_copy.wait()


def shards(
    table_slab,
    request_rows,
    owner_counts,
    item_slots,
    regroup_counts,
    history_lengths,
    w_proj,
    bias_proj,
    gain_in,
    gain_mid,
    rel_bias,
    w_out,
):
    peers = lax.axis_size("seq")
    tables = lax.axis_size("table")
    slab_rows, width = table_slab.shape
    tokens = item_slots.shape[1]
    half = CAP // 2
    msg_rows = (request_rows.shape[1] // LANES + 1 + 7) // 8 * 8
    micro = tokens // 2 // MB_TOK
    hbm = pl.BlockSpec(memory_space=pltpu.HBM)
    dma = pltpu.SemaphoreType.DMA
    return pl.pallas_call(
        functools.partial(kernel, (peers, tables)),
        out_shape=jax.ShapeDtypeStruct((1, tokens, width), BF16),
        in_specs=[hbm] * 12,
        out_specs=hbm,
        scratch_shapes=[
            pltpu.VMEM(request_rows.shape, jnp.int32),
            pltpu.SMEM(owner_counts.shape, jnp.int32),
            pltpu.VMEM(item_slots.shape, jnp.int32),
            pltpu.SMEM(regroup_counts.shape, jnp.int32),
            pltpu.SMEM(history_lengths.shape, jnp.int32),
            pltpu.VMEM(bias_proj.shape, F32),
            pltpu.VMEM(gain_in.shape, F32),
            pltpu.VMEM(gain_mid.shape, F32),
            pltpu.VMEM(rel_bias.shape, F32),
            pltpu.VMEM((slab_rows, width), BF16),
            pltpu.VMEM((2, width, 4 * width), BF16),
            pltpu.VMEM((2, width, width), BF16),
            pltpu.VMEM((2, 16, width), F32),
            pltpu.VMEM((tables, msg_rows, LANES), jnp.int32),
            pltpu.VMEM((peers, tokens // LANES, LANES), jnp.int32),
            pltpu.VMEM((tables, half, LANES), jnp.int32),
            pltpu.VMEM((tables, half, width), BF16),
            pltpu.VMEM((peers, 2, tables, half, width), BF16),
            pltpu.VMEM((2, HEADS, LANES, 2 * LANES), F32),
            pltpu.VMEM((micro, MB_TOK // 2, MB_TOK + MB_TOK // 2), F32),
            pltpu.VMEM((2, tokens // 2, width), BF16),
            dma((13,)),
            dma((3,)),
            dma((3,)),
            dma((tables,)),
            dma((tables,)),
            dma((peers,)),
            dma((peers,)),
            dma((tables,)),
            dma((tables,)),
            dma((peers, tables)),
            dma((peers, tables)),
            dma((peers, tables)),
            dma((peers, tables)),
            dma((1,)),
            dma((1,)),
        ],
        compiler_params=pltpu.CompilerParams(
            collective_id=0, has_side_effects=True, vmem_limit_bytes=58 * 1024 * 1024
        ),
        name="hstu_window",
    )(
        table_slab,
        request_rows,
        owner_counts,
        item_slots,
        regroup_counts,
        history_lengths,
        w_proj,
        bias_proj,
        gain_in,
        gain_mid,
        rel_bias,
        w_out,
    )


def solution(mesh):
    in_specs = (
        P("table", None),
        P(("seq", "table"), None),
        P(("seq", "table"), None),
        P(("seq", "table"), None),
        P("table", None, None),
        P(("seq", "table"), None),
        P("section", None, None),
        P("section", None),
        P("section", None),
        P("section", None),
        P("section", None, None),
        P("section", None, None),
    )
    out_specs = P("section", ("seq", "table"), None)
    return jax.shard_map(shards, mesh=mesh, in_specs=in_specs, out_specs=out_specs, check_vma=False)
```

```python
import functools

import jax
import jax.numpy as jnp
from jax import lax
from jax.experimental import pallas as pl
from jax.experimental.pallas import tpu as pltpu
from jax.sharding import PartitionSpec as P

HEADS = 4
MB_TOK = 256
CAP = 64
LANES = 128
MESH = pl.DeviceIdType.MESH
F32 = jnp.float32
BF16 = jnp.bfloat16


def iota(shape, axis):
    return lax.broadcasted_iota(jnp.int32, shape, axis)


def normalise(values):
    center = values - jnp.mean(values, axis=-1, keepdims=True)
    spread = jnp.mean(center * center, axis=-1, keepdims=True)
    return center * lax.rsqrt(spread + 1e-05)


def silu_of_half(half):
    return half + half * jnp.tanh(half)


def kernel(
    dims,
    slab_hbm,
    req_hbm,
    counts_hbm,
    slots_hbm,
    plan_hbm,
    lengths_hbm,
    wp_hbm,
    bias_hbm,
    gin_hbm,
    gmid_hbm,
    rel_hbm,
    wo_hbm,
    out_ref,
    req_ref,
    counts_smem,
    slots_ref,
    plan_smem,
    lengths_smem,
    bias_ref,
    gin_ref,
    gmid_ref,
    rel_ref,
    slab,
    wp,
    wo,
    par,
    msg,
    flat,
    ids,
    gath,
    rows,
    grid,
    mask,
    made,
    local_sem,
    wsend,
    wrecv,
    msend,
    mrecv,
    fsend,
    frecv,
    rsend,
    rrecv,
    xsend,
    xrecv,
    ssend,
    srecv,
    osend,
    orecv,
):
    peers, tables = dims
    half = CAP // 2
    width = slab.shape[1]
    span = LANES
    tokens = slots_ref.shape[1]
    mine = tokens // 2
    micro = mine // MB_TOK
    listed = req_ref.shape[1] // LANES
    slab_rows = slab.shape[0]
    block_rows = 2 * tables * half
    users = lengths_smem.shape[1]
    head_size = width // HEADS
    c = lax.axis_index("section")
    s = lax.axis_index("seq")
    t = lax.axis_index("table")
    sib = (1 - c, s, t)

    def table_peer(k):
        if tables & (tables - 1):
            return lax.rem(t + k, tables)
        flipped = 0
        bit = 1
        while bit < tables:
            own = lax.rem(t // bit, 2)
            turn = lax.rem(k // bit, 2)
            flipped = flipped + bit * (own + turn - 2 * own * turn)
            bit = 2 * bit
        return flipped

    def seq_peer(k):
        return lax.rem(s + k, peers)

    def remote(src, dst, send, recv, to):
        return pltpu.make_async_remote_copy(
            src_ref=src,
            dst_ref=dst,
            send_sem=send,
            recv_sem=recv,
            device_id=to,
            device_id_type=MESH,
        )

    small = [
        pltpu.make_async_copy(source, place, local_sem.at[3 + k])
        for k, (source, place) in enumerate(
            (
                (counts_hbm, counts_smem),
                (req_hbm, req_ref),
                (slots_hbm, slots_ref),
                (bias_hbm, bias_ref),
                (gin_hbm, gin_ref),
                (gmid_hbm, gmid_ref),
                (rel_hbm, rel_ref),
                (lengths_hbm, lengths_smem),
                (plan_hbm, plan_smem),
            )
        )
    ]
    for copy in small:
        copy.start()
    slab_copy = pltpu.make_async_copy(slab_hbm, slab, local_sem.at[0])
    wp_copy = pltpu.make_async_copy(wp_hbm.at[0], wp.at[c], local_sem.at[1])
    wo_copy = pltpu.make_async_copy(wo_hbm.at[0], wo.at[c], local_sem.at[2])
    slab_copy.start()
    wp_copy.start()
    wo_copy.start()

    barrier = pltpu.get_barrier_semaphore()

    def greet_table(k, carry):
        pl.semaphore_signal(barrier, inc=1, device_id=(c, s, table_peer(k)), device_id_type=MESH)
        return carry

    def greet_seq(k, carry):
        pl.semaphore_signal(barrier, inc=1, device_id=(c, seq_peer(k), t), device_id_type=MESH)
        return carry

    lax.fori_loop(1, tables, greet_table, 0)
    lax.fori_loop(1, peers, greet_seq, 0)
    pl.semaphore_signal(barrier, inc=1, device_id=sib, device_id_type=MESH)

    for copy in small:
        copy.wait()

    for k in range(listed):
        msg[t, k : k + 1, :] = req_ref[0:1, k * LANES : (k + 1) * LANES]
    lane = iota((1, LANES), 1)
    first_row = jnp.zeros((1, LANES), jnp.int32)
    limit = jnp.int32(0)
    limits = []
    for o in range(tables):
        first_row = jnp.where(lane == o, limit, first_row)
        limit = limit + counts_smem[0, o]
        limits.append(limit)
    msg[t, listed : listed + 1, :] = first_row

    for k in range(tokens // LANES):
        slot = slots_ref[0:1, k * LANES : (k + 1) * LANES]
        owner = jnp.zeros((1, LANES), jnp.int32)
        first = jnp.zeros((1, LANES), jnp.int32)
        for o in range(tables):
            past = slot >= limits[o]
            owner = owner + jnp.where(past, 1, 0)
            first = jnp.where(past, limits[o], first)
        place = slot - first
        place = place + owner * half + jnp.where(place >= half, (tables - 1) * half, 0)
        flat[s, k : k + 1, :] = place

    for k in range(4):
        par[c, k : k + 1, :] = bias_ref[0:1, k * width : (k + 1) * width] * 0.5
    par[c, 4:5, :] = gin_ref[...]
    par[c, 5:6, :] = gmid_ref[...]
    for k in range(HEADS):
        par[c, 8 + k : 9 + k, 0:span] = rel_ref[0, k : k + 1, :] * 0.5

    pl.semaphore_wait(barrier, (tables - 1) + (peers - 1) + 1)

    def ask(k):
        return remote(msg.at[t], msg.at[t], msend.at[k], mrecv.at[t], (c, s, table_peer(k)))

    def ask_step(k, carry):
        ask(k).start()
        return carry

    lax.fori_loop(1, tables, ask_step, 0)

    def tell(k):
        return remote(flat.at[s], flat.at[s], fsend.at[k], frecv.at[s], (c, seq_peer(k), t))

    def tell_step(k, carry):
        tell(k).start()
        return carry

    lax.fori_loop(1, peers, tell_step, 0)
    par_copy = remote(par.at[c], par.at[c], wsend.at[0], wrecv.at[0], sib)
    wp_send = remote(wp_hbm.at[0], wp.at[c], wsend.at[1], wrecv.at[1], sib)
    wo_send = remote(wo_hbm.at[0], wo.at[c], wsend.at[2], wrecv.at[2], sib)
    par_copy.start()
    wp_send.start()
    wo_send.start()

    lower = MB_TOK // 2
    for m in range(micro):
        row_owner = jnp.zeros((1, MB_TOK), jnp.int32)
        col_owner = jnp.zeros((MB_TOK, 1), jnp.int32)
        place_row = iota((1, MB_TOK), 1)
        place_col = iota((MB_TOK, 1), 0)
        end = jnp.int32(0)
        for u in range(users):
            end = end + lengths_smem[c * micro + m, u]
            row_owner = row_owner + jnp.where(place_row >= end, 1, 0)
            col_owner = col_owner + jnp.where(place_col >= end, 1, 0)
        top = (col_owner[:lower] == row_owner[:, :lower]) & (place_row[:, :lower] <= place_col[:lower])
        low = (col_owner[lower:] == row_owner) & (place_row <= place_col[lower:])
        mask[m, :, 0:lower] = jnp.where(top, 1.0, 0.0)
        mask[m, :, lower:] = jnp.where(low, 1.0, 0.0)

    def hear(k, carry):
        o = table_peer(k)
        remote(msg.at[o], msg.at[o], msend.at[k], mrecv.at[o], (c, s, o)).wait_recv()
        return carry

    lax.fori_loop(1, tables, hear, 0)

    def read_ids(o, carry):
        firsts = msg[o, listed : listed + 1, :]
        first = jnp.sum(jnp.where(lane == t, firsts, 0).astype(F32), axis=1, keepdims=True)
        want = first.astype(jnp.int32) + c * half + iota((half, LANES), 0)
        total = jnp.zeros((half, LANES), F32)
        for k in range(listed):
            listed_row = msg[o, k : k + 1, :].astype(F32)
            total = total + jnp.where(iota((half, LANES), 1) + k * LANES == want, listed_row, 0.0)
        found = jnp.sum(total, axis=1, keepdims=True).astype(jnp.int32)
        ids[o] = jnp.broadcast_to(found, (half, LANES))
        return carry

    lax.fori_loop(0, tables, read_ids, 0)
    slab_copy.wait()
    wanted = ids[...].reshape(tables * half, LANES)
    spots = iota((tables * half, LANES), 1)
    picks = jnp.concatenate(
        [jnp.where(wanted == spots + k * LANES, 1.0, 0.0).astype(BF16) for k in range(slab_rows // LANES)],
        axis=1,
    )
    looked_up = jnp.dot(picks, slab[...], preferred_element_type=F32).astype(BF16)
    gath[...] = looked_up.reshape(tables, half, width)

    def serve(k):
        o = table_peer(k)
        return remote(gath.at[o], rows.at[s, c, t], rsend.at[k], rrecv.at[t], (c, s, o))

    def serve_step(k, carry):
        serve(k).start()
        return carry

    lax.fori_loop(1, tables, serve_step, 0)
    rows[s, c, t] = gath[t]

    def across(k, o):
        place = rows.at[s, c, o]
        return remote(place, place, xsend.at[k, o], xrecv.at[s, o], (c, seq_peer(k), t))

    def beside(source, o):
        place = rows.at[source, c, o]
        return remote(place, place, ssend.at[source, o], srecv.at[source, o], sib)

    def pass_on(o):
        def one(k, carry):
            across(k, o).start()
            return carry

        lax.fori_loop(1, peers, one, 0)
        beside(s, o).start()

    pass_on(t)

    wp_copy.wait()
    wo_copy.wait()
    par_copy.wait_recv()
    for layer in range(2):
        for head in range(HEADS):
            rel_row = jnp.broadcast_to(par[layer, 8 + head : 9 + head, 0:span], (span, span))
            rel_col = jnp.sum(
                jnp.where(iota((span, span), 0) == iota((span, span), 1), rel_row, 0.0), axis=1, keepdims=True
            )
            turned = jnp.where(
                iota((span, 2 * span), 0) + iota((span, 2 * span), 1) == span, rel_col, 0.0
            )
            base = jnp.broadcast_to(jnp.sum(turned, axis=0, keepdims=True), (span, 2 * span))
            grid[layer, head] = pltpu.roll(base, 0, 1, stride=1, stride_axis=0)

    def heard(k, carry):
        source = seq_peer(k)
        remote(flat.at[source], flat.at[source], fsend.at[k], frecv.at[source], (c, source, t)).wait_recv()
        return carry

    lax.fori_loop(1, peers, heard, 0)

    def second(k):
        o = table_peer(k)

        def one(i, carry):
            source = seq_peer(i)
            place = rows.at[source, c, o]
            remote(place, place, xsend.at[i, o], xrecv.at[source, o], (c, source, t)).wait_recv()
            beside(source, o).start()
            return carry

        lax.fori_loop(1, peers, one, 0)

    def collect(k, carry):
        o = table_peer(k)
        remote(gath.at[o], rows.at[s, c, o], rsend.at[k], rrecv.at[o], (c, s, o)).wait_recv()
        pass_on(o)
        second(k - 1)
        return carry

    lax.fori_loop(1, tables, collect, 0)

    chunk = mine
    places = iota((chunk, LANES), 0) + c * mine
    total = jnp.zeros((chunk, LANES), F32)
    for source in range(peers):
        sent_first = jnp.int32(0)
        got_first = jnp.int32(0)
        for other in range(peers):
            sent_first = sent_first + jnp.where(other < s, plan_smem[0, source, other], 0)
            if other < source:
                got_first = got_first + plan_smem[0, other, s]
        number = plan_smem[0, source, s]
        for k in range(tokens // LANES):
            rank = lane + k * LANES - sent_first
            inside = (rank >= 0) & (rank < number)
            position = jnp.where(inside, rank + got_first, -1)
            value = (flat[source, k : k + 1, :] + source * block_rows).astype(F32)
            total = total + jnp.where(places == position, value, 0.0)
    index = jnp.sum(total, axis=1, keepdims=True).astype(jnp.int32)

    second(tables - 1)

    def arrived(i, carry):
        source = i // tables
        o = lax.rem(i, tables)
        place = rows.at[source, 1 - c, o]
        remote(place, place, ssend.at[source, o], srecv.at[source, o], sib).wait_recv()
        return carry

    lax.fori_loop(0, peers * tables, arrived, 0)

    hidden = jnp.zeros((mine, width), F32)
    for source in range(peers):
        picks = jnp.where(index == iota((1, block_rows), 1) + source * block_rows, 1.0, 0.0).astype(BF16)
        hidden = hidden + jnp.dot(
            picks, rows[source].reshape(block_rows, width), preferred_element_type=F32
        )

    wp_send.wait_recv()
    wo_send.wait_recv()

    out_copy = remote(
        made.at[1 - c], out_ref.at[0, pl.ds(c * mine, mine)], osend.at[0], orecv.at[0], sib
    )
    own_copy = pltpu.make_async_copy(
        made.at[c], out_ref.at[0, pl.ds(c * mine, mine)], local_sem.at[12]
    )
    for layer in range(2):
        normed = (normalise(hidden) * par[layer, 4:5, :]).astype(BF16)
        parts = []
        for k in range(4):
            projected = jnp.dot(
                normed, wp[layer, :, k * width : (k + 1) * width], preferred_element_type=F32
            )
            parts.append(silu_of_half(projected * 0.5 + par[layer, k : k + 1, :]).astype(BF16))
        gate, value, query, key = parts
        scale = 0.5 * head_size ** (-0.5)
        contract = (((1,), (1,)), ((), ()))
        batches = []
        for m in range(micro):
            r0, r1, r2 = m * MB_TOK, m * MB_TOK + lower, (m + 1) * MB_TOK
            heads = []
            for head in range(HEADS):
                f0, f1 = head * head_size, (head + 1) * head_size
                k_all = key[r0:r2, f0:f1]
                v_all = value[r0:r2, f0:f1]
                top = lax.dot_general(
                    query[r0:r1, f0:f1], k_all[:lower], contract, preferred_element_type=F32
                )
                low = lax.dot_general(query[r1:r2, f0:f1], k_all, contract, preferred_element_type=F32)
                top = silu_of_half(top * scale + grid[layer, head, :, lower:])
                low = silu_of_half(low * scale + grid[layer, head])
                top = (top * mask[m, :, 0:lower]).astype(BF16)
                low = (low * mask[m, :, lower:]).astype(BF16)
                heads.append(
                    jnp.concatenate(
                        [
                            jnp.dot(top, v_all[:lower], preferred_element_type=F32),
                            jnp.dot(low, v_all, preferred_element_type=F32),
                        ],
                        axis=0,
                    )
                )
            batches.append(jnp.concatenate(heads, axis=1))
        attended = jnp.concatenate(batches, axis=0)
        gated = (normalise(attended) * par[layer, 5:6, :] * gate.astype(F32)).astype(BF16)
        state = (hidden + jnp.dot(gated, wo[layer], preferred_element_type=F32)).astype(BF16)
        hidden = state.astype(F32)

        made[layer] = state

        @pl.when(c == layer)
        def _():
            own_copy.start()

        @pl.when(c != layer)
        def _():
            out_copy.start()

    def sent_table(k, carry):
        ask(k).wait_send()
        serve(k).wait_send()
        return carry

    def sent_seq(k, carry):
        tell(k).wait_send()
        return carry

    def sent_across(i, carry):
        across(1 + i // tables, lax.rem(i, tables)).wait_send()
        return carry

    def sent_beside(i, carry):
        beside(i // tables, lax.rem(i, tables)).wait_send()
        return carry

    lax.fori_loop(1, tables, sent_table, 0)
    lax.fori_loop(1, peers, sent_seq, 0)
    lax.fori_loop(0, (peers - 1) * tables, sent_across, 0)
    lax.fori_loop(0, peers * tables, sent_beside, 0)
    par_copy.wait_send()
    wp_send.wait_send()
    wo_send.wait_send()
    own_copy.wait()
    out_copy.wait()


def shards(
    table_slab,
    request_rows,
    owner_counts,
    item_slots,
    regroup_counts,
    history_lengths,
    w_proj,
    bias_proj,
    gain_in,
    gain_mid,
    rel_bias,
    w_out,
):
    peers = lax.axis_size("seq")
    tables = lax.axis_size("table")
    slab_rows, width = table_slab.shape
    tokens = item_slots.shape[1]
    half = CAP // 2
    msg_rows = (request_rows.shape[1] // LANES + 1 + 7) // 8 * 8
    micro = tokens // 2 // MB_TOK
    hbm = pl.BlockSpec(memory_space=pltpu.HBM)
    dma = pltpu.SemaphoreType.DMA
    return pl.pallas_call(
        functools.partial(kernel, (peers, tables)),
        out_shape=jax.ShapeDtypeStruct((1, tokens, width), BF16),
        in_specs=[hbm] * 12,
        out_specs=hbm,
        scratch_shapes=[
            pltpu.VMEM(request_rows.shape, jnp.int32),
            pltpu.SMEM(owner_counts.shape, jnp.int32),
            pltpu.VMEM(item_slots.shape, jnp.int32),
            pltpu.SMEM(regroup_counts.shape, jnp.int32),
            pltpu.SMEM(history_lengths.shape, jnp.int32),
            pltpu.VMEM(bias_proj.shape, F32),
            pltpu.VMEM(gain_in.shape, F32),
            pltpu.VMEM(gain_mid.shape, F32),
            pltpu.VMEM(rel_bias.shape, F32),
            pltpu.VMEM((slab_rows, width), BF16),
            pltpu.VMEM((2, width, 4 * width), BF16),
            pltpu.VMEM((2, width, width), BF16),
            pltpu.VMEM((2, 16, width), F32),
            pltpu.VMEM((tables, msg_rows, LANES), jnp.int32),
            pltpu.VMEM((peers, tokens // LANES, LANES), jnp.int32),
            pltpu.VMEM((tables, half, LANES), jnp.int32),
            pltpu.VMEM((tables, half, width), BF16),
            pltpu.VMEM((peers, 2, tables, half, width), BF16),
            pltpu.VMEM((2, HEADS, LANES, 2 * LANES), F32),
            pltpu.VMEM((micro, MB_TOK // 2, MB_TOK + MB_TOK // 2), F32),
            pltpu.VMEM((2, tokens // 2, width), BF16),
            dma((13,)),
            dma((3,)),
            dma((3,)),
            dma((tables,)),
            dma((tables,)),
            dma((peers,)),
            dma((peers,)),
            dma((tables,)),
            dma((tables,)),
            dma((peers, tables)),
            dma((peers, tables)),
            dma((peers, tables)),
            dma((peers, tables)),
            dma((1,)),
            dma((1,)),
        ],
        compiler_params=pltpu.CompilerParams(
            collective_id=0, has_side_effects=True, vmem_limit_bytes=58 * 1024 * 1024
        ),
        name="hstu_window",
    )(
        table_slab,
        request_rows,
        owner_counts,
        item_slots,
        regroup_counts,
        history_lengths,
        w_proj,
        bias_proj,
        gain_in,
        gain_mid,
        rel_bias,
        w_out,
    )


def solution(mesh):
    in_specs = (
        P("table", None),
        P(("seq", "table"), None),
        P(("seq", "table"), None),
        P(("seq", "table"), None),
        P("table", None, None),
        P(("seq", "table"), None),
        P("section", None, None),
        P("section", None),
        P("section", None),
        P("section", None),
        P("section", None, None),
        P("section", None, None),
    )
    out_specs = P("section", ("seq", "table"), None)
    return jax.shard_map(shards, mesh=mesh, in_specs=in_specs, out_specs=out_specs, check_vma=False)
```
